256 devices in a mesh: row: 8 (over x_hi, y), col: 16 (over z, core), dp: 2 (over x_lo).
Axes of the slice: x: 4 (x_hi: 2, x_lo: 2; x = x_hi * 2 + x_lo), y: 4, z: 8, core: 2. Of those that a mesh axis runs over, the one named last changes fastest.
Arguments:
- tokens: bfloat16 [1536, 5120], P(('col', 'dp'), 'row'), may hold values from -6 to 6
- w_gate: bfloat16 [5120, 14336], P('row', 'col'), may hold values from -0.078125 to 0.078125
- w_up: bfloat16 [5120, 14336], P('row', 'col'), may hold values from -0.078125 to 0.078125
- w_down: bfloat16 [14336, 5120], P('col', 'row'), may hold values from -0.046875 to 0.046875
- grad_out: bfloat16 [1536, 5120], P(('col', 'dp'), 'row'), may hold values from -6 to 6
Outputs:
- mixed: bfloat16 [1536, 5120], P(('col', 'dp'), 'row')
- grad_tokens: bfloat16 [1536, 5120], P(('col', 'dp'), 'row')
- grad_w_gate: bfloat16 [5120, 14336], P(('row', 'dp'), 'col')
- grad_w_up: bfloat16 [5120, 14336], P(('row', 'dp'), 'col')
- grad_w_down: bfloat16 [14336, 5120], P('col', ('row', 'dp'))
The draws below stay inside these ranges and needn't reach their ends.
All inputs are finite; a program needn't handle non-finite values.
Results may differ from the reference program's by a relative error of at most 0.005.
Values may be sent and summed in bfloat16 or wider, within the bound.
A program may use at most 128 MiB of HBM per device.

```python
import jax
import jax.numpy as jnp

D = 5120
FF = 14336
TOKENS = 1536


def spiked(result, own_key, source, target, shards_of, factor):
    def block_of(axis_at):
        return (jnp.arange(result.shape[axis_at]) // (result.shape[axis_at] // shards_of)).reshape((-1,) + (1,) * (result.ndim - 1 - axis_at))

    first = jax.random.permutation(own_key, shards_of)[block_of(target)]
    second = (block_of(target) + shards_of // 2) % shards_of
    return jnp.where((block_of(source) == first) | (block_of(source) == second), factor * result, result)


def block_scale(stream_key, dims, cuts, smallest, high):
    gain, own = 1.0, jax.random.fold_in(stream_key, 6)
    for axis_at, blocks in cuts:
        steps = jnp.exp(jax.random.uniform(jax.random.fold_in(own, axis_at), (blocks,), jnp.float32, smallest / len(cuts), high / len(cuts)))
        gain = gain * jnp.repeat(steps, dims[axis_at] // blocks).reshape([-1 if axis == axis_at else 1 for axis in range(len(dims))])
    return gain


def gaussian(own_key, extent, deviation, limit, split=(), held_as=jnp.bfloat16):
    level = block_scale(own_key, extent, split, -0.22, 0.18) if split else 1.0
    result = jax.random.normal(own_key, extent, jnp.float32) * deviation * level
    return jnp.minimum(jnp.maximum(result, -limit), limit).astype(held_as)


def gaussian_with(key, shape, scale, reach, cuts, heavy, held_as=jnp.bfloat16):
    drawn = scale * jax.random.normal(key, shape, jnp.float32)
    if cuts:
        drawn = drawn * block_scale(key, shape, cuts, -0.22, 0.18)
    return jnp.clip(spiked(drawn, jax.random.fold_in(key, 3), *heavy), -reach, reach).astype(held_as)


def setup_inputs(seed: int = 0) -> dict:
    key_of = jax.random.split(jax.random.key(seed), 6)
    tokens = gaussian(key_of[0], (TOKENS, D), 1.0, 6.0, ((0, 32), (1, 8)))
    w_gate = gaussian(key_of[1], (D, FF), D ** -0.5, 0.078125, ((0, 8), (1, 16)))
    w_up = gaussian(key_of[2], (D, FF), D ** -0.5, 0.078125, ((0, 8), (1, 16)))
    w_down = gaussian(key_of[3], (FF, D), FF ** -0.5, 0.046875, ((0, 16), (1, 8)))
    grad_out = gaussian_with(key_of[4], (TOKENS, D), 1.0, 6.0, ((0, 32), (1, 8)), (0, 1, 32, 2.75))
    return dict(tokens=tokens, w_gate=w_gate, w_up=w_up, w_down=w_down, grad_out=grad_out)


def reference(tokens, w_gate, w_up, w_down, grad_out):
    gate = jnp.dot(tokens, w_gate, preferred_element_type=jnp.float32)
    up = jnp.dot(tokens, w_up, preferred_element_type=jnp.float32)
    sig = jax.nn.sigmoid(gate)
    hidden = (gate * sig * up).astype(jnp.bfloat16)
    mixed = jnp.dot(hidden, w_down, preferred_element_type=jnp.float32).astype(jnp.bfloat16)
    grad_hidden = jnp.dot(grad_out, w_down.T, preferred_element_type=jnp.float32)
    grad_up = (grad_hidden * gate * sig).astype(jnp.bfloat16)
    grad_gate = (grad_hidden * up * sig * (1.0 + gate * (1.0 - sig))).astype(jnp.bfloat16)
    grad_tokens = (jnp.dot(grad_gate, w_gate.T, preferred_element_type=jnp.float32)
                   + jnp.dot(grad_up, w_up.T, preferred_element_type=jnp.float32)).astype(jnp.bfloat16)
    grad_w_gate = jnp.dot(tokens.T, grad_gate, preferred_element_type=jnp.float32).astype(jnp.bfloat16)
    grad_w_up = jnp.dot(tokens.T, grad_up, preferred_element_type=jnp.float32).astype(jnp.bfloat16)
    grad_w_down = jnp.dot(hidden.T, grad_out, preferred_element_type=jnp.float32).astype(jnp.bfloat16)
    return mixed, grad_tokens, grad_w_gate, grad_w_up, grad_w_down
```

```python
import functools

import jax
import jax.numpy as jnp
from jax import lax
from jax.experimental import pallas as pl
from jax.experimental.pallas import tpu as pltpu
from jax.sharding import PartitionSpec as P

MESH = pl.DeviceIdType.MESH
BF16, F32 = jnp.bfloat16, jnp.float32
NY, NZ = 4, 8
CUT = 512


def dot(a, b):
    return jnp.dot(a, b, preferred_element_type=F32)


def dot_last(a, b):
    return lax.dot_general(a, b, (((1,), (1,)), ((), ())), preferred_element_type=F32)


def dot_first(a, b):
    return lax.dot_general(a, b, (((0,), (0,)), ((), ())), preferred_element_type=F32)


def flat(x):
    return x.reshape((-1, x.shape[-1]))


class Links:
    def __init__(self, send, recv):
        self.send, self.recv = send, recv
        self.n_send = self.n_recv = 0
        self.started = []

    def slots(self, n=1):
        first = self.n_recv
        self.n_recv += n
        return first

    def copy(self, src, dst, slot, to):
        c = pltpu.make_async_remote_copy(
            src_ref=src,
            dst_ref=dst,
            send_sem=self.send.at[self.n_send],
            recv_sem=self.recv.at[slot],
            device_id=to,
            device_id_type=MESH,
        )
        self.n_send += 1
        return c

    def put(self, src, dst, slot, to):
        c = self.copy(src, dst, slot, to)
        c.start()
        self.started.append((c, None))

    def put_or_keep(self, src, dst, slot, to, away):
        c = self.copy(src, dst, slot, to)

        @pl.when(away == 1)
        def _():
            c.start()

        @pl.when(away == 0)
        def _():
            pltpu.make_async_copy(src, dst, self.recv.at[slot]).start()

        self.started.append((c, away))

    def arrived(self, dst, slot):
        pltpu.make_async_copy(dst, dst, self.recv.at[slot]).wait()

    def finish(self):
        for c, away in self.started:
            if away is None:
                c.wait_send()
            else:
                pl.when(away == 1)(c.wait_send)


def kernel(
    tok, wg_h, wu_h, wd_h, go, mixed_o, gt_o, gwg_o, gwu_o, gwd_o,
    tok_a, go_a, wg, wu, wd, tok_t,
    g_p, g_f, g_x, g_s, g_y, u_p, u_f, u_y, u_s, u_x,
    h1_p, h1_f, h1_x, h1_s, h1_y, h2_p, h2_f, h2_y, h2_s, h2_x,
    gate_v, up_v, sig_v, hid_a, gg_a, gu_a,
    part1, part2, pair1, pair2, zs1, zs2, zr1, zr2,
    dw_f, dw_s, dw_r, gw_f, gw_s, gw_r,
    send, recv, loc,
):
    row, col, l = lax.axis_index("row"), lax.axis_index("col"), lax.axis_index("dp")
    h, y = row // NY, lax.rem(row, NY)
    z, k = col // 2, lax.rem(col, 2)
    l1 = l + h - 2 * l * h

    def dev(hh, yy, zz, kk, ll):
        return (hh * NY + yy, zz * 2 + kk, ll)

    def ys(d):
        return lax.rem(y + d, NY)

    def zs(d):
        return lax.rem(z + d + NZ, NZ)

    over_y = [None] + [dev(h, ys(d), z, k, l) for d in (1, 2, 3)]
    over_x = dev(1 - h, y, z, k, 1 - l)
    twin = (row, col, 1 - l)
    core = dev(h, y, z, 1 - k, l)

    loads = []
    for i, (src, dst) in enumerate(((wg_h, wg), (wu_h, wu), (wd_h, wd))):
        c = pltpu.make_async_copy(src, dst, loc.at[i])
        c.start()
        loads.append(c)

    barrier = pltpu.get_barrier_semaphore()
    friends = [over_x, twin, core, dev(h, y, z, 1 - k, 1 - l)] + over_y[1:]
    for d in range(1, NZ):
        for ll in (l, 1 - l):
            friends.append(dev(h, y, zs(d), k, ll))
    for to in friends:
        pl.semaphore_signal(barrier, inc=1, device_id=to, device_id_type=MESH)
    pl.semaphore_wait(barrier, len(friends))

    net = Links(send, recv)

    side = 1 - 2 * k
    gathers = [(src, dst, net.slots(16)) for src, dst in ((tok, tok_a), (go, go_a))]

    def gather_put(dst, base, origin, to):
        net.put(dst.at[origin], dst.at[origin], base + origin, to)

    for src, dst, base in gathers:
        for to in (dev(h, y, zs(side), k, l1), dev(h, y, zs(-side), k, l1), dev(h, y, z, 1 - k, l1)):
            net.put(src, dst.at[col], base + col, to)
        net.put_or_keep(src, dst.at[col], base + col, dev(h, y, z, k, l1), h)
    for step in range(1, 5):
        for src, dst, base in gathers:
            far = zs(-side * step) * 2 + k
            net.arrived(dst.at[far], base + far)
            if step < 4:
                gather_put(dst, base, far, dev(h, y, zs(side), k, l))
            gather_put(dst, base, far, core)
            if step < 4:
                near = zs(side * step) * 2 + k
                net.arrived(dst.at[near], base + near)
                if step < 3:
                    gather_put(dst, base, near, dev(h, y, zs(-side), k, l))
                gather_put(dst, base, near, core)
    for src, dst, base in gathers:
        net.arrived(dst.at[col], base + col)
        for zz in range(NZ):
            other = zz * 2 + 1 - k
            net.arrived(dst.at[other], base + other)

    def rows_of(ref, half, q):
        return flat(ref[pl.ds(half * 8 + q * 4, 4)])

    def x_first_send(ref, mm, p, x):
        slot = net.slots(2)
        for q in range(2):
            out = mm(rows_of(ref, 1 - h, q))
            p[pl.ds(2 * q, 2)] = out.astype(BF16).reshape((2, 96, -1))
            net.put(p.at[pl.ds(2 * q, 2)], x.at[pl.ds(2 * q, 2)], slot + q, over_x)
        return slot

    def x_first_own(ref, mm, f):
        for q in range(2):
            f[pl.ds(2 * q, 2)] = mm(rows_of(ref, h, q)).reshape((2, 96, -1))

    def x_first_pass(f, x, s, yr, slot):
        for q in range(2):
            net.arrived(x.at[pl.ds(2 * q, 2)], slot + q)
        for i in range(4):
            s[i] = (f[i] + x[i].astype(F32)).astype(BF16)
        slot = net.slots(3)
        for d in (1, 3, 2):
            net.put(s.at[ys(d)], yr.at[d - 1], slot + d - 1, over_y[d])
        return slot

    def x_first_sum(f, x, yr, slot):
        total = f[y] + x[y].astype(F32)
        for d in (1, 3, 2):
            net.arrived(yr.at[d - 1], slot + d - 1)
            total = total + yr[d - 1].astype(F32)
        return total

    def y_first_send(ref, mm, p, f, yr):
        for half in range(2):
            for q in range(2):
                out = mm(rows_of(ref, half, q)).reshape((2, 96, -1))
                f[half, pl.ds(2 * q, 2)] = out
                p[half, pl.ds(2 * q, 2)] = out.astype(BF16)
        slot = net.slots(3)
        for d in (1, 3, 2):
            net.put(p.at[:, ys(d)], yr.at[d - 1], slot + d - 1, over_y[d])
        return slot

    def y_first_pass(f, yr, s, x, slot):
        for d in (1, 3, 2):
            net.arrived(yr.at[d - 1], slot + d - 1)
        total = f[1 - h, y]
        for d in (1, 3, 2):
            total = total + yr[d - 1, 1 - h].astype(F32)
        s[...] = total.astype(BF16)
        slot = net.slots()
        net.put(s, x, slot, over_x)
        return slot

    def y_first_sum(f, yr, x, slot):
        total = f[h, y]
        for d in (1, 3, 2):
            total = total + yr[d - 1, h].astype(F32)
        net.arrived(x, slot)
        return total + x[...].astype(F32)

    def mm_g(a):
        return dot(a, wg[...])

    def mm_u(a):
        return dot(a, wu[...])

    def mm_h1(a):
        return dot_last(a, wd[:CUT])

    def mm_h2(a):
        return dot_last(a, wd[CUT:])

    loads[0].wait()
    g1 = x_first_send(tok_a, mm_g, g_p, g_x)
    loads[1].wait()
    u1 = y_first_send(tok_a, mm_u, u_p, u_f, u_y)
    x_first_own(tok_a, mm_g, g_f)
    loads[2].wait()
    h11 = x_first_send(go_a, mm_h1, h1_p, h1_x)
    h21 = y_first_send(go_a, mm_h2, h2_p, h2_f, h2_y)
    x_first_own(go_a, mm_h1, h1_f)
    g2 = x_first_pass(g_f, g_x, g_s, g_y, g1)
    u2 = y_first_pass(u_f, u_y, u_s, u_x, u1)
    tok_t[...] = flat(tok_a[...]).T
    gate = x_first_sum(g_f, g_x, g_y, g2)
    up = y_first_sum(u_f, u_y, u_x, u2)
    sig = jax.nn.sigmoid(gate)
    gate_v[...] = gate
    up_v[...] = up
    sig_v[...] = sig
    hid_a[h, y] = (gate * sig * up).astype(BF16)

    def spread(buf, lo, hi):
        cols = pl.ds(lo, hi - lo)
        slot = net.slots(8)

        def at(hh, yy):
            return buf.at[hh, yy, :, cols]

        for to in (over_x, over_y[1], over_y[3], over_y[2]):
            net.put(at(h, y), at(h, y), slot + row, to)
        return at, slot

    def relay_y(piece):
        at, slot = piece
        net.arrived(at(1 - h, y), slot + (1 - h) * NY + y)
        for d in (1, 3, 2):
            net.put(at(1 - h, y), at(1 - h, y), slot + (1 - h) * NY + y, over_y[d])

    def relay_y_rest(piece):
        at, slot = piece
        for d in (1, 3, 2):
            for hh in (h, 1 - h):
                net.arrived(at(hh, ys(d)), slot + hh * NY + ys(d))

    def relay_x(piece):
        at, slot = piece
        for d in (1, 3, 2):
            net.arrived(at(h, ys(d)), slot + h * NY + ys(d))
            net.put(at(h, ys(d)), at(h, ys(d)), slot + h * NY + ys(d), over_x)

    def relay_x_rest(piece):
        at, slot = piece
        for d in range(4):
            net.arrived(at(1 - h, ys(d)), slot + (1 - h) * NY + ys(d))

    width = hid_a.shape[-1]
    hid0 = spread(hid_a, 0, CUT)
    hid1 = spread(hid_a, CUT, width)
    h12 = x_first_pass(h1_f, h1_x, h1_s, h1_y, h11)
    h22 = y_first_pass(h2_f, h2_y, h2_s, h2_x, h21)
    relay_y(hid1)
    relay_x(hid0)
    for at, total in (
        (pl.ds(0, CUT), x_first_sum(h1_f, h1_x, h1_y, h12)),
        (pl.ds(CUT, width - CUT), y_first_sum(h2_f, h2_y, h2_x, h22)),
    ):
        gate, up, sig = gate_v[:, at], up_v[:, at], sig_v[:, at]
        gu_a[h, y, :, at] = (total * gate * sig).astype(BF16)
        gg_a[h, y, :, at] = (total * up * sig * (1.0 + gate * (1.0 - sig))).astype(BF16)
    gg0 = spread(gg_a, 0, CUT)
    gu0 = spread(gu_a, 0, CUT)
    gg1 = spread(gg_a, CUT, width)
    gu1 = spread(gu_a, CUT, width)

    relay_x_rest(hid0)
    relay_y_rest(hid1)

    def down_grad(lo, hi):
        for j in range(lo, hi, 128):
            at = pl.ds(j, 128)
            both = dot_first(flat(flat_rows(hid_a, at)), flat(go_a[...]))
            first, second = both[:, :320], both[:, 320:]
            mine = jnp.where(l == 0, first, second)
            dw_f[at] = mine
            dw_s[at] = jnp.where(l == 0, second, first).astype(BF16)
        slot = net.slots()
        at = pl.ds(lo, hi - lo)
        net.put(dw_s.at[at], dw_r.at[at], slot, twin)
        return slot, at

    def flat_rows(buf, at):
        return buf[:, :, :, at].reshape((8, 96, -1))

    dw0 = down_grad(0, CUT)
    relay_y(gu0)
    relay_x(gg0)
    dw1 = down_grad(CUT, width)

    def pair_send(part, pair):
        slot = net.slots()
        net.put(part.at[:, 1 - k], pair, slot, core)
        return slot

    def pair_pass(part, pair, zsend, zrecv, slot):
        net.arrived(pair, slot)
        for zz in range(NZ):
            zsend[zz] = (part[zz, k] + pair[zz]).astype(BF16)
        slot = net.slots(NZ)
        for d in (4, 3, 5, 2, 6, 1, 7):
            net.put(zsend.at[zs(d)], zrecv.at[d], slot + d, dev(h, y, zs(d), k, l1))
        net.put_or_keep(zsend.at[z], zrecv.at[0], slot, dev(h, y, z, k, l1), h)
        return slot

    def z_sum(zrecv, slot):
        total = None
        for d in range(NZ):
            net.arrived(zrecv.at[d], slot + d)
            block = zrecv[d].astype(F32)
            total = block if total is None else total + block
        return total.astype(BF16)

    def rows4(buf, i):
        half, q = i // 2, i % 2
        return flat(buf[half, pl.ds(2 * q, 2)])

    for i in range(4):
        part1[pl.ds(2 * i, 2)] = dot(rows4(hid_a, i), wd[...]).reshape((2, 2, 48, -1))
    m1 = pair_send(part1, pair1)
    relay_y(gu1)
    relay_x(gg1)

    def weight_grad(buf, first, lo, hi):
        at = pl.ds(lo, hi - lo)
        to = pl.ds(first + lo, hi - lo)
        for mine in (False, True):
            base = (l if mine else 1 - l) * 320
            for q in range(2):
                left = tok_t[pl.ds(pl.multiple_of(base + q * 160, 32), 160)]
                out = dot(left, flat(buf[:, :, :, at].reshape((8, 96, -1))))
                if mine:
                    gw_f[pl.ds(q * 160, 160), to] = out
                else:
                    gw_s[pl.ds(q * 160, 160), to] = out.astype(BF16)
            if not mine:
                slot = net.slots()
                net.put(gw_s.at[:, to], gw_r.at[:, to], slot, twin)
        return slot, to

    relay_x_rest(gg0)
    wg0 = weight_grad(gg_a, 0, 0, CUT)
    relay_y_rest(gu0)
    wu0 = weight_grad(gu_a, width, 0, CUT)
    m2 = pair_pass(part1, pair1, zs1, zr1, m1)
    relay_x_rest(gg1)
    wg1 = weight_grad(gg_a, 0, CUT, width)
    relay_y_rest(gu1)
    wu1 = weight_grad(gu_a, width, CUT, width)
    for i in range(4):
        out = dot_last(rows4(gg_a, i), wg[...]) + dot_last(rows4(gu_a, i), wu[...])
        part2[pl.ds(2 * i, 2)] = out.reshape((2, 2, 48, -1))
    t1 = pair_send(part2, pair2)
    for slot, at in (dw0, dw1):
        net.arrived(dw_r.at[at], slot)
        gwd_o[at] = (dw_f[at] + dw_r[at].astype(F32)).astype(BF16)
    t2 = pair_pass(part2, pair2, zs2, zr2, t1)
    mixed_o[...] = z_sum(zr1, m2)
    for out, (slot, at), lo, hi in (
        (gwg_o, wg0, 0, CUT), (gwu_o, wu0, 0, CUT), (gwg_o, wg1, CUT, width), (gwu_o, wu1, CUT, width),
    ):
        net.arrived(gw_r.at[:, at], slot)
        out[:, pl.ds(lo, hi - lo)] = (gw_f[:, at] + gw_r[:, at].astype(F32)).astype(BF16)
    gt_o[...] = z_sum(zr2, t2)
    net.finish()


def per_device(tokens, w_gate, w_up, w_down, grad_out):
    n_tok, d = tokens.shape
    f = w_gate.shape[1]
    rest = f - CUT

    def x_first(w):
        return [
            pltpu.VMEM((4, 96, w), BF16),
            pltpu.VMEM((4, 96, w), F32),
            pltpu.VMEM((4, 96, w), BF16),
            pltpu.VMEM((4, 96, w), BF16),
            pltpu.VMEM((3, 96, w), BF16),
        ]

    def y_first(w):
        return [
            pltpu.VMEM((2, 4, 96, w), BF16),
            pltpu.VMEM((2, 4, 96, w), F32),
            pltpu.VMEM((3, 2, 96, w), BF16),
            pltpu.VMEM((96, w), BF16),
            pltpu.VMEM((96, w), BF16),
        ]

    scratch = [
        pltpu.VMEM((16, n_tok, d), BF16),
        pltpu.VMEM((16, n_tok, d), BF16),
        pltpu.VMEM(w_gate.shape, BF16),
        pltpu.VMEM(w_up.shape, BF16),
        pltpu.VMEM(w_down.shape, BF16),
        pltpu.VMEM((d, 16 * n_tok), BF16),
        *x_first(f),
        *y_first(f),
        *x_first(CUT),
        *y_first(rest),
        *[pltpu.VMEM((96, f), F32)] * 3,
        *[pltpu.VMEM((2, 4, 96, f), BF16)] * 3,
        *[pltpu.VMEM((8, 2, n_tok, d), F32)] * 2,
        *[pltpu.VMEM((8, n_tok, d), F32)] * 2,
        *[pltpu.VMEM((8, n_tok, d), BF16)] * 4,
        pltpu.VMEM((f, d // 2), F32),
        pltpu.VMEM((f, d // 2), BF16),
        pltpu.VMEM((f, d // 2), BF16),
        pltpu.VMEM((d // 2, 2 * f), F32),
        pltpu.VMEM((d // 2, 2 * f), BF16),
        pltpu.VMEM((d // 2, 2 * f), BF16),
        pltpu.SemaphoreType.DMA((160,)),
        pltpu.SemaphoreType.DMA((160,)),
        pltpu.SemaphoreType.DMA((3,)),
    ]
    vmem, hbm = pl.BlockSpec(memory_space=pltpu.VMEM), pl.BlockSpec(memory_space=pl.ANY)
    return pl.pallas_call(
        kernel,
        out_shape=(
            jax.ShapeDtypeStruct((n_tok, d), BF16),
            jax.ShapeDtypeStruct((n_tok, d), BF16),
            jax.ShapeDtypeStruct((d // 2, f), BF16),
            jax.ShapeDtypeStruct((d // 2, f), BF16),
            jax.ShapeDtypeStruct((f, d // 2), BF16),
        ),
        in_specs=[vmem, hbm, hbm, hbm, vmem],
        out_specs=(vmem,) * 5,
        scratch_shapes=scratch,
        compiler_params=pltpu.CompilerParams(
            collective_id=0, has_side_effects=True, vmem_limit_bytes=62 * 2**20
        ),
        name="swiglu",
    )(tokens, w_gate, w_up, w_down, grad_out)


def solution(mesh):
    placed = (
        P(("col", "dp"), "row"),
        P("row", "col"),
        P("row", "col"),
        P("col", "row"),
        P(("col", "dp"), "row"),
    )
    return jax.shard_map(
        per_device,
        mesh=mesh,
        in_specs=placed,
        out_specs=(
            P(("col", "dp"), "row"),
            P(("col", "dp"), "row"),
            P(("row", "dp"), "col"),
            P(("row", "dp"), "col"),
            P("col", ("row", "dp")),
        ),
        check_vma=False,
    )
```

```python
import functools

import jax
import jax.numpy as jnp
from jax import lax
from jax.experimental import pallas as pl
from jax.experimental.pallas import tpu as pltpu
from jax.sharding import PartitionSpec as P

MESH = pl.DeviceIdType.MESH
BF16, F32 = jnp.bfloat16, jnp.float32
NY, NZ = 4, 8
CUT = 512


def dot(a, b):
    return jnp.dot(a, b, preferred_element_type=F32)


def dot_last(a, b):
    return lax.dot_general(a, b, (((1,), (1,)), ((), ())), preferred_element_type=F32)


def dot_first(a, b):
    return lax.dot_general(a, b, (((0,), (0,)), ((), ())), preferred_element_type=F32)


def flat(x):
    return x.reshape((-1, x.shape[-1]))


class Links:
    def __init__(self, send, late, recv):
        self.send, self.late, self.recv = send, late, recv
        self.n_send = self.n_recv = 0
        self.started = []

    def slots(self, n=1):
        first = self.n_recv
        self.n_recv += n
        return first

    def copy(self, src, dst, slot, to):
        c = pltpu.make_async_remote_copy(
            src_ref=src,
            dst_ref=dst,
            send_sem=self.send.at[self.n_send],
            recv_sem=self.recv.at[slot],
            device_id=to,
            device_id_type=MESH,
        )
        self.n_send += 1
        return c

    def put(self, src, dst, slot, to):
        c = self.copy(src, dst, slot, to)
        c.start()
        self.started.append((c, None))

    def put_or_keep(self, src, dst, slot, to, away):
        c = self.copy(src, dst, slot, to)

        @pl.when(away == 1)
        def _():
            c.start()

        @pl.when(away == 0)
        def _():
            pltpu.make_async_copy(src, dst, self.recv.at[slot]).start()

        self.started.append((c, away))

    def aside(self, src, dst, slot, to):
        pltpu.make_async_remote_copy(
            src_ref=src,
            dst_ref=dst,
            send_sem=self.late.at[slot - self.late_first],
            recv_sem=self.recv.at[slot],
            device_id=to,
            device_id_type=MESH,
        ).start()

    def aside_sent(self, src, dst, slot, to):
        pltpu.make_async_remote_copy(
            src_ref=src,
            dst_ref=dst,
            send_sem=self.late.at[slot - self.late_first],
            recv_sem=self.recv.at[slot],
            device_id=to,
            device_id_type=MESH,
        ).wait_send()

    def arrived(self, dst, slot):
        pltpu.make_async_copy(dst, dst, self.recv.at[slot]).wait()

    def finish(self, last=0):
        done, self.started = self.started[: len(self.started) - last], self.started[len(self.started) - last :]
        for c, away in done:
            if away is None:
                c.wait_send()
            else:
                pl.when(away == 1)(c.wait_send)


def kernel(
    tok, wg_h, wu_h, wd_h, go, mixed_o, gt_o, gwg_o, gwu_o, gwd_o,
    tok_a, go_a, wg, wu, wd, tok_t, go_t,
    g_p, g_f, g_x, g_s, g_y, u_p, u_f, u_y, u_s, u_x,
    h1_p, h1_f, h1_x, h1_s, h1_y, h2_p, h2_f, h2_y, h2_s, h2_x,
    gate_v, up_v, sig_v, hid_a, gr_a,
    part1, part2, pair1, pair2, zs1, zs2, zr1, zr2, mixed_v, gt_v,
    gw_f, gw_s, gw_r,
    send, late, recv, loc,
):
    row, col, l = lax.axis_index("row"), lax.axis_index("col"), lax.axis_index("dp")
    h, y = row // NY, lax.rem(row, NY)
    z, k = col // 2, lax.rem(col, 2)
    l1 = l + h - 2 * l * h

    def dev(hh, yy, zz, kk, ll):
        return (hh * NY + yy, zz * 2 + kk, ll)

    def ys(d):
        return lax.rem(y + d, NY)

    def zs(d):
        return lax.rem(z + d + NZ, NZ)

    over_y = [None] + [dev(h, ys(d), z, k, l) for d in (1, 2, 3)]
    over_x = dev(1 - h, y, z, k, 1 - l)
    twin = (row, col, 1 - l)
    core = dev(h, y, z, 1 - k, l)

    loads = []
    for i, (src, dst) in enumerate(((wg_h, wg), (wu_h, wu), (wd_h, wd))):
        c = pltpu.make_async_copy(src, dst, loc.at[i])
        c.start()
        loads.append(c)

    barrier = pltpu.get_barrier_semaphore()
    friends = [over_x, twin, core, dev(h, y, z, 1 - k, 1 - l)] + over_y[1:]
    for d in range(1, NZ):
        for ll in (l, 1 - l):
            friends.append(dev(h, y, zs(d), k, ll))
    for to in friends:
        pl.semaphore_signal(barrier, inc=1, device_id=to, device_id_type=MESH)
    pl.semaphore_wait(barrier, len(friends))

    net = Links(send, late, recv)

    side = 1 - 2 * k
    tok_g, go_g = [(dst, net.slots(16)) for dst in (tok_a, go_a)]

    def gather_put(gather, origin, to):
        dst, base = gather
        net.put(dst.at[origin], dst.at[origin], base + origin, to)

    def gather_start(src, gather):
        dst, base = gather
        for to in (dev(h, y, zs(side), k, l1), dev(h, y, zs(-side), k, l1), dev(h, y, z, 1 - k, l1)):
            net.put(src, dst.at[col], base + col, to)
        net.put_or_keep(src, dst.at[col], base + col, dev(h, y, z, k, l1), h)

    def gather_step(gather, step):
        dst, base = gather
        far = zs(-side * step) * 2 + k
        net.arrived(dst.at[far], base + far)
        if step < 4:
            gather_put(gather, far, dev(h, y, zs(side), k, l))
        gather_put(gather, far, core)
        if step < 4:
            near = zs(side * step) * 2 + k
            net.arrived(dst.at[near], base + near)
            if step < 3:
                gather_put(gather, near, dev(h, y, zs(-side), k, l))
            gather_put(gather, near, core)

    def gathered(gather, zz):
        dst, base = gather
        if zz is z:
            net.arrived(dst.at[col], base + col)
        other = zz * 2 + 1 - k
        net.arrived(dst.at[other], base + other)
        return flat(dst[pl.ds(zz * 2, 2)])

    def x_first_block(out, zz, sums):
        f, p, x, slot = sums
        hi, yi = zz // NY, lax.rem(zz, NY)

        @pl.when(hi == h)
        def _():
            f[yi] = out

        @pl.when(hi != h)
        def _():
            p[yi] = out.astype(BF16)
            net.aside(p.at[yi], x.at[yi], slot + yi, over_x)

    def x_first_pass(f, x, s, yr, slot):
        first = net.slots(3)
        for d in (2, 1, 3):
            i = ys(d)
            net.arrived(x.at[i], slot + i)
            s[i] = (f[i] + x[i].astype(F32)).astype(BF16)
            net.put(s.at[i], yr.at[d - 1], first + d - 1, over_y[d])
        net.arrived(x.at[y], slot + y)
        return first

    def x_first_sum(f, x, yr, slot):
        total = f[y] + x[y].astype(F32)
        for d in (1, 3, 2):
            net.arrived(yr.at[d - 1], slot + d - 1)
            total = total + yr[d - 1].astype(F32)
        return total

    def y_first_block(out, zz, sums):
        f, p, yr, slot = sums
        hi, yi = zz // NY, lax.rem(zz, NY)
        f[hi, yi] = out

        @pl.when(yi != y)
        def _():
            p[hi, yi] = out.astype(BF16)
            d = lax.rem(yi - y + NY, NY) - 1
            net.aside(p.at[hi, yi], yr.at[d, hi], slot + 2 * d + hi, dev(h, yi, z, k, l))

    def y_first_pass(f, yr, s, x, slot):
        total = f[1 - h, y]
        for d in (1, 3, 2):
            net.arrived(yr.at[d - 1, 1 - h], slot + 2 * (d - 1) + 1 - h)
            total = total + yr[d - 1, 1 - h].astype(F32)
        s[...] = total.astype(BF16)
        first = net.slots()
        net.put(s, x, first, over_x)
        return first

    def y_first_sum(f, yr, x, slot1, slot2):
        total = f[h, y]
        for d in (1, 3, 2):
            net.arrived(yr.at[d - 1, h], slot1 + 2 * (d - 1) + h)
            total = total + yr[d - 1, h].astype(F32)
        net.arrived(x, slot2)
        return total + x[...].astype(F32)

    net.late_first = net.n_recv
    g1, u1, h11, h21 = net.slots(4), net.slots(6), net.slots(4), net.slots(6)

    def block_gu(zz):
        a = gathered(tok_g, zz)
        y_first_block(dot(a, wu[...]), zz, (u_f, u_p, u_y, u1))
        x_first_block(dot(a, wg[...]), zz, (g_f, g_p, g_x, g1))

    def block_h(zz):
        a = gathered(go_g, zz)
        y_first_block(dot_last(a, wd[CUT:]), zz, (h2_f, h2_p, h2_y, h21))
        x_first_block(dot_last(a, wd[:CUT]), zz, (h1_f, h1_p, h1_x, h11))

    def chips(step):
        return (zs(-side * step), zs(side * step)) if step < 4 else (zs(4),)

    gather_start(tok, tok_g)
    for c in loads:
        c.wait()
    gather_step(tok_g, 1)
    gather_start(go, go_g)
    block_gu(z)
    for step in (2, 3, 4):
        gather_step(tok_g, step)
        gather_step(go_g, step - 1)
        for zz in chips(step - 1):
            block_gu(zz)
    gather_step(go_g, 4)
    block_gu(zs(4))
    block_h(z)
    for zz in chips(1):
        block_h(zz)
    g2 = x_first_pass(g_f, g_x, g_s, g_y, g1)
    u2 = y_first_pass(u_f, u_y, u_s, u_x, u1)
    for step in (2, 3, 4):
        for zz in chips(step):
            block_h(zz)
    tok_t[...] = flat(tok_a[...]).T
    gate = x_first_sum(g_f, g_x, g_y, g2)
    up = y_first_sum(u_f, u_y, u_x, u1, u2)
    sig = jax.nn.sigmoid(gate)
    gate_v[...] = gate
    up_v[...] = up
    sig_v[...] = sig
    hid_a[0, h, y] = (gate * sig * up).astype(BF16)

    class Spread:
        def __init__(self, buf, lo, hi):
            self.buf, self.cols = buf, pl.ds(lo, hi - lo)
            self.base = net.slots(10)
            self.put(h, y, over_x)
            self.put(h, y, over_y[1])
            self.put(h, y, over_y[3])

        def at(self, hh, yy, half=None):
            rows = pl.ds(0, 96) if half is None else pl.ds(48 * half, 48)
            return self.buf.at[:, hh, yy, rows, self.cols]

        def slot(self, hh, yy, half=None):
            return self.base + (8 + hh if half == 1 else hh * NY + yy)

        def put(self, hh, yy, to, half=None):
            ref = self.at(hh, yy, half)
            net.put(ref, ref, self.slot(hh, yy, half), to)

        def wait(self, hh, yy, half=None):
            net.arrived(self.at(hh, yy, half), self.slot(hh, yy, half))

        def across(self, hh, also_x=False):
            for d, half in ((3, 0), (1, 1)):
                self.wait(hh, ys(d))
                self.put(hh, ys(d), over_y[4 - d], half)
                if also_x:
                    self.put(hh, ys(d), over_x)

    class XThenY(Spread):
        def relay1(self):
            self.wait(1 - h, y)
            self.put(1 - h, y, over_y[1])
            self.put(1 - h, y, over_y[3])

        def relay2(self):
            self.across(h)

        def relay3(self):
            self.across(1 - h)

        def rest(self):
            for hh in (h, 1 - h):
                for half in (0, 1):
                    self.wait(hh, ys(2), half)

    class YThenX(Spread):
        def relay1(self):
            self.across(h, True)

        def relay2(self):
            for half in (0, 1):
                self.wait(h, ys(2), half)
                self.put(h, ys(2), over_x, half)

        def rest(self):
            for d in (0, 1, 3):
                self.wait(1 - h, ys(d))
            for half in (0, 1):
                self.wait(1 - h, ys(2), half)

    width = hid_a.shape[-1]
    hid0 = XThenY(hid_a, 0, CUT)
    hid1 = YThenX(hid_a, CUT, width)
    h12 = x_first_pass(h1_f, h1_x, h1_s, h1_y, h11)
    h22 = y_first_pass(h2_f, h2_y, h2_s, h2_x, h21)
    go_t[...] = flat(go_a[...]).T
    hid0.relay1()
    hid1.relay1()
    hid0.relay2()

    def grads(at, total):
        gate, up, sig = gate_v[:, at], up_v[:, at], sig_v[:, at]
        gr_a[1, h, y, :, at] = (total * gate * sig).astype(BF16)
        gr_a[0, h, y, :, at] = (total * up * sig * (1.0 + gate * (1.0 - sig))).astype(BF16)

    grads(pl.ds(0, CUT), x_first_sum(h1_f, h1_x, h1_y, h12))
    gr0 = XThenY(gr_a, 0, CUT)
    grads(pl.ds(CUT, width - CUT), y_first_sum(h2_f, h2_y, h2_x, h21, h22))
    gr1 = YThenX(gr_a, CUT, width)
    hid1.relay2()
    hid0.relay3()
    gr0.relay1()

    def weight_grad(left, buf, first, lo, hi, mine):
        at, to = pl.ds(lo, hi - lo), pl.ds(first + lo, hi - lo)
        base = (l if mine else 1 - l) * 320
        right = buf[:, :, :, at].reshape((8 * 96, hi - lo))
        for q in range(2):
            out = dot(left[pl.ds(pl.multiple_of(base + q * 160, 32), 160)], right)
            if mine:
                gw_f[pl.ds(q * 160, 160), to] = out
            else:
                gw_s[pl.ds(q * 160, 160), to] = out.astype(BF16)
        if not mine:
            slot = net.slots()
            net.put(gw_s.at[:, to], gw_r.at[:, to], slot, twin)
            return slot, to

    def weight_out(out, lo, hi, sent):
        slot, at = sent
        net.arrived(gw_r.at[:, at], slot)
        out[:, pl.ds(lo, hi - lo)] = (gw_f[:, at] + gw_r[:, at].astype(F32)).astype(BF16)

    def pair_send(part, pair, lo, hi):
        slot, at = net.slots(), pl.ds(lo, hi - lo)
        net.put(part.at[at, 1 - k], pair.at[at], slot, core)
        return slot, at

    def pair_pass(part, pair, zsend, zrecv, sent):
        for slot, at in sent:
            net.arrived(pair.at[at], slot)
        for zz in range(NZ):
            zsend[zz] = (part[zz, k] + pair[zz]).astype(BF16)
        slot = net.slots(NZ)
        for d in (4, 3, 5, 2, 6, 1, 7):
            net.put(zsend.at[zs(d)], zrecv.at[d], slot + d, dev(h, y, zs(d), k, l))
        return slot

    def z_sum(part, pair, zrecv, slot, out):
        total = part[z, k] + pair[z]
        for d in (1, 7, 2, 6, 3, 5, 4):
            net.arrived(zrecv.at[d], slot + d)
            total = total + zrecv[d].astype(F32)
        zrecv[0] = total.astype(BF16)
        net.put_or_keep(zrecv.at[0], out, slot, twin, h)
        return out, slot

    def rows4(buf, i, at):
        return buf[i // 2, pl.ds(2 * (i % 2), 2), :, at].reshape((192, -1))

    hid, gg, gu = hid_a.at[0], gr_a.at[0], gr_a.at[1]
    hid0.rest()
    hid1.rest()
    dw = weight_grad(go_t, hid, 2 * width, 0, width, False)
    gr1.relay1()
    gr0.relay2()
    gr1.relay2()
    gr0.relay3()
    sent = []
    for i in range(4):
        part1[pl.ds(2 * i, 2)] = dot(rows4(hid, i, pl.ds(0, width)), wd[...]).reshape((2, 2, 48, -1))
        sent.append(pair_send(part1, pair1, 2 * i, 2 * i + 2))
    gr0.rest()
    wg0 = weight_grad(tok_t, gg, 0, 0, CUT, False)
    m2 = pair_pass(part1, pair1, zs1, zr1, sent)
    wu0 = weight_grad(tok_t, gu, width, 0, CUT, False)

    def token_grad(i, lo, hi):
        at = pl.ds(lo, hi - lo)
        out = dot_last(rows4(gg, i, at), wg[:, at]) + dot_last(rows4(gu, i, at), wu[:, at])
        return out.reshape((2, 2, 48, -1))

    for i in range(4):
        part2[pl.ds(2 * i, 2)] = token_grad(i, 0, CUT)
    gr1.rest()
    sent = []
    for i in range(4):
        part2[pl.ds(2 * i, 2)] += token_grad(i, CUT, width)
        sent.append(pair_send(part2, pair2, 2 * i, 2 * i + 2))
    wg1 = weight_grad(tok_t, gg, 0, CUT, width, False)
    wu1 = weight_grad(tok_t, gu, width, CUT, width, False)
    t2 = pair_pass(part2, pair2, zs2, zr2, sent)
    for first, n, p, x in (
        (g1, 4, g_p.at[0], g_x.at[0]),
        (u1, 6, u_p.at[0, 0], u_y.at[0, 0]),
        (h11, 4, h1_p.at[0], h1_x.at[0]),
        (h21, 6, h2_p.at[0, 0], h2_y.at[0, 0]),
    ):
        for i in range(n):
            net.aside_sent(p, x, first + i, over_x)
    net.finish(25)
    weight_grad(go_t, hid, 2 * width, 0, width, True)
    weight_out(gwd_o, 0, width, dw)
    mixed = z_sum(part1, pair1, zr1, m2, mixed_v)
    weight_grad(tok_t, gg, 0, 0, width, True)
    weight_grad(tok_t, gu, width, 0, width, True)
    weight_out(gwg_o, 0, CUT, wg0)
    weight_out(gwu_o, 0, CUT, wu0)
    grad = z_sum(part2, pair2, zr2, t2, gt_v)
    weight_out(gwg_o, CUT, width, wg1)
    weight_out(gwu_o, CUT, width, wu1)
    for o, (v, slot) in ((mixed_o, mixed), (gt_o, grad)):
        net.arrived(v, slot)
        o[...] = v[...]
    net.finish()


def copy_out(*refs):
    for i in range(5):
        refs[5 + i][...] = refs[i][...]


def per_device(tokens, w_gate, w_up, w_down, grad_out):
    n_tok, d = tokens.shape
    f = w_gate.shape[1]
    rest = f - CUT

    def x_first(w):
        return [
            pltpu.VMEM((4, 96, w), BF16),
            pltpu.VMEM((4, 96, w), F32),
            pltpu.VMEM((4, 96, w), BF16),
            pltpu.VMEM((4, 96, w), BF16),
            pltpu.VMEM((3, 96, w), BF16),
        ]

    def y_first(w):
        return [
            pltpu.VMEM((2, 4, 96, w), BF16),
            pltpu.VMEM((2, 4, 96, w), F32),
            pltpu.VMEM((3, 2, 96, w), BF16),
            pltpu.VMEM((96, w), BF16),
            pltpu.VMEM((96, w), BF16),
        ]

    scratch = [
        pltpu.VMEM((16, n_tok, d), BF16),
        pltpu.VMEM((16, n_tok, d), BF16),
        pltpu.VMEM(w_gate.shape, BF16),
        pltpu.VMEM(w_up.shape, BF16),
        pltpu.VMEM(w_down.shape, BF16),
        *[pltpu.VMEM((d, 16 * n_tok), BF16)] * 2,
        *x_first(f),
        *y_first(f),
        *x_first(CUT),
        *y_first(rest),
        *[pltpu.VMEM((96, f), F32)] * 3,
        pltpu.VMEM((1, 2, 4, 96, f), BF16),
        pltpu.VMEM((2, 2, 4, 96, f), BF16),
        *[pltpu.VMEM((8, 2, n_tok, d), F32)] * 2,
        *[pltpu.VMEM((8, n_tok, d), F32)] * 2,
        *[pltpu.VMEM((8, n_tok, d), BF16)] * 4,
        *[pltpu.VMEM((n_tok, d), BF16)] * 2,
        pltpu.VMEM((d // 2, 3 * f), F32),
        pltpu.VMEM((d // 2, 3 * f), BF16),
        pltpu.VMEM((d // 2, 3 * f), BF16),
        pltpu.SemaphoreType.DMA((160,)),
        pltpu.SemaphoreType.DMA((20,)),
        pltpu.SemaphoreType.DMA((160,)),
        pltpu.SemaphoreType.DMA((3,)),
    ]
    vmem, hbm = pl.BlockSpec(memory_space=pltpu.VMEM), pl.BlockSpec(memory_space=pl.ANY)
    results = pl.pallas_call(
        kernel,
        out_shape=(
            jax.ShapeDtypeStruct((n_tok, d), BF16),
            jax.ShapeDtypeStruct((n_tok, d), BF16),
            jax.ShapeDtypeStruct((d // 2, f), BF16),
            jax.ShapeDtypeStruct((d // 2, f), BF16),
            jax.ShapeDtypeStruct((d // 2, f), BF16),
        ),
        in_specs=[vmem, hbm, hbm, hbm, vmem],
        out_specs=(vmem,) * 5,
        scratch_shapes=scratch,
        compiler_params=pltpu.CompilerParams(
            collective_id=0, has_side_effects=True, vmem_limit_bytes=62 * 2**20
        ),
        name="swiglu",
    )(tokens, w_gate, w_up, w_down, grad_out)
    mixed, grad_tokens, grad_gate, grad_up, grad_down = pl.pallas_call(
        copy_out,
        out_shape=tuple(jax.ShapeDtypeStruct(r.shape, r.dtype) for r in results),
        in_specs=[vmem] * 5,
        out_specs=(vmem,) * 5,
        name="copy_out",
    )(*results)
    return mixed, grad_tokens, grad_gate, grad_up, grad_down.T


def solution(mesh):
    placed = (
        P(("col", "dp"), "row"),
        P("row", "col"),
        P("row", "col"),
        P("col", "row"),
        P(("col", "dp"), "row"),
    )
    return jax.shard_map(
        per_device,
        mesh=mesh,
        in_specs=placed,
        out_specs=(
            P(("col", "dp"), "row"),
            P(("col", "dp"), "row"),
            P(("row", "dp"), "col"),
            P(("row", "dp"), "col"),
            P("col", ("row", "dp")),
        ),
        check_vma=False,
    )
```

```python
import functools

import jax
import jax.numpy as jnp
from jax import lax
from jax.experimental import pallas as pl
from jax.experimental.pallas import tpu as pltpu
from jax.sharding import PartitionSpec as P

MESH = pl.DeviceIdType.MESH
BF16, F32 = jnp.bfloat16, jnp.float32
NY, NZ = 4, 8
CUT = 512


def dot(a, b):
    return jnp.dot(a, b, preferred_element_type=F32)


def dot_last(a, b):
    return lax.dot_general(a, b, (((1,), (1,)), ((), ())), preferred_element_type=F32)


def dot_first(a, b):
    return lax.dot_general(a, b, (((0,), (0,)), ((), ())), preferred_element_type=F32)


def flat(x):
    return x.reshape((-1, x.shape[-1]))


class Links:
    def __init__(self, send, late, recv):
        self.send, self.late, self.recv = send, late, recv
        self.n_send = self.n_recv = 0
        self.started = []

    def slots(self, n=1):
        first = self.n_recv
        self.n_recv += n
        return first

    def copy(self, src, dst, slot, to):
        c = pltpu.make_async_remote_copy(
            src_ref=src,
            dst_ref=dst,
            send_sem=self.send.at[self.n_send],
            recv_sem=self.recv.at[slot],
            device_id=to,
            device_id_type=MESH,
        )
        self.n_send += 1
        return c

    def put(self, src, dst, slot, to):
        c = self.copy(src, dst, slot, to)
        c.start()
        self.started.append((c, None))

    def put_or_keep(self, src, dst, slot, to, away):
        c = self.copy(src, dst, slot, to)

        @pl.when(away == 1)
        def _():
            c.start()

        @pl.when(away == 0)
        def _():
            pltpu.make_async_copy(src, dst, self.recv.at[slot]).start()

        self.started.append((c, away))

    def aside(self, src, dst, slot, to, sem=None):
        pltpu.make_async_remote_copy(
            src_ref=src,
            dst_ref=dst,
            send_sem=self.late.at[slot - self.late_first if sem is None else sem],
            recv_sem=self.recv.at[slot],
            device_id=to,
            device_id_type=MESH,
        ).start()

    def aside_sent(self, src, dst, slot, to, sem=None):
        pltpu.make_async_remote_copy(
            src_ref=src,
            dst_ref=dst,
            send_sem=self.late.at[slot - self.late_first if sem is None else sem],
            recv_sem=self.recv.at[slot],
            device_id=to,
            device_id_type=MESH,
        ).wait_send()

    def arrived(self, dst, slot):
        pltpu.make_async_copy(dst, dst, self.recv.at[slot]).wait()

    def finish(self, last=0):
        done, self.started = self.started[: len(self.started) - last], self.started[len(self.started) - last :]
        for c, away in done:
            if away is None:
                c.wait_send()
            else:
                pl.when(away == 1)(c.wait_send)


def kernel(
    tok, wg_h, wu_h, wd_h, go, mixed_o, gt_o, gwg_o, gwu_o, gwd_o,
    tok_a, go_a, wg, wu, wd, tok_t, go_t,
    g_p, g_f, g_x, g_s, g_y, u_p, u_f, u_y, u_s, u_x,
    h1_p, h1_f, h1_x, h1_s, h1_y, h2_p, h2_f, h2_y, h2_s, h2_x,
    gate_v, up_v, sig_v, hid_a, gr_a,
    part1, part2, pair1, pair2, zs1, zs2, zr1, zr2, mixed_v, gt_v,
    gw_f, gw_s, gw_r,
    send, late, recv, loc,
):
    row, col, l = lax.axis_index("row"), lax.axis_index("col"), lax.axis_index("dp")
    h, y = row // NY, lax.rem(row, NY)
    z, k = col // 2, lax.rem(col, 2)

    def dev(hh, yy, zz, kk, ll):
        return (hh * NY + yy, zz * 2 + kk, ll)

    def ys(d):
        return lax.rem(y + d, NY)

    def zs(d):
        return lax.rem(z + d + NZ, NZ)

    over_y = [None] + [dev(h, ys(d), z, k, l) for d in (1, 2, 3)]
    over_x = dev(1 - h, y, z, k, 1 - l)
    twin = (row, col, 1 - l)
    core = dev(h, y, z, 1 - k, l)

    loads = []
    for i, (src, dst) in enumerate(((wg_h, wg), (wu_h, wu), (wd_h, wd))):
        c = pltpu.make_async_copy(src, dst, loc.at[i])
        c.start()
        loads.append(c)

    barrier = pltpu.get_barrier_semaphore()
    friends = [over_x, twin, core] + over_y[1:]
    for d in (1, 2, 6, 7):
        friends.append(dev(h, y, zs(d), k, l))
    for to in friends:
        pl.semaphore_signal(barrier, inc=1, device_id=to, device_id_type=MESH)
    pl.semaphore_wait(barrier, len(friends))

    net = Links(send, late, recv)

    side = 1 - 2 * k
    tok_g, go_g = [(dst, net.slots(16)) for dst in (tok_a, go_a)]

    def gather_put(gather, origin, to):
        dst, base = gather
        net.put(dst.at[origin], dst.at[origin], base + origin, to)

    def gather_start(src, gather):
        dst, base = gather
        net.put_or_keep(src, dst.at[col], base + col, twin, h)

    def gather_share(gather):
        dst, base = gather
        net.arrived(dst.at[col], base + col)
        gather_put(gather, col, core)
        for d in (2 * side, -2 * side, side, -side):
            gather_put(gather, col, dev(h, y, zs(d), k, l))

    def gather_pass(gather, steps, targets):
        origin = zs(steps) * 2 + k
        dst, base = gather
        net.arrived(dst.at[origin], base + origin)
        for d in targets:
            gather_put(gather, origin, dev(h, y, zs(d), k, l))
        gather_put(gather, origin, core)

    def gather_two(gather):
        gather_pass(gather, -2 * side, (2 * side, side))
        gather_pass(gather, 2 * side, (-side,))

    def gather_one(gather):
        gather_pass(gather, -side, ())
        gather_pass(gather, side, ())

    def gather_rest(gather):
        for d in (-3 * side, 3 * side, 4):
            gather_pass(gather, d, ())

    def gathered(gather, zz):
        dst, base = gather
        other = zz * 2 + 1 - k
        net.arrived(dst.at[other], base + other)
        return flat(dst[pl.ds(zz * 2, 2)])

    def x_first_block(out, zz, sums):
        f, p, x, slot = sums
        hi, yi = zz // NY, lax.rem(zz, NY)

        @pl.when(hi == h)
        def _():
            f[yi] = out

        @pl.when(hi != h)
        def _():
            p[yi] = out.astype(BF16)
            net.aside(p.at[yi], x.at[yi], slot + yi, over_x)

    def x_first_pass(f, x, s, yr, slot):
        first = net.slots(3)
        for d in (2, 1, 3):
            i = ys(d)
            net.arrived(x.at[i], slot + i)
            s[i] = (f[i] + x[i].astype(F32)).astype(BF16)
            net.put(s.at[i], yr.at[d - 1], first + d - 1, over_y[d])
        net.arrived(x.at[y], slot + y)
        return first

    def x_first_relay(zz, sums, to):
        f, p, x, slot = sums
        s, yr, first, sem = to
        hi, yi = zz // NY, lax.rem(zz, NY)

        @pl.when(hi == h)
        def _():
            net.arrived(x.at[yi], slot + yi)

            @pl.when(yi != y)
            def _():
                d = lax.rem(yi - y + NY, NY) - 1
                s[yi] = (f[yi] + x[yi].astype(F32)).astype(BF16)
                net.aside(s.at[yi], yr.at[d], first + d, dev(h, yi, z, k, l), sem + d)

    def x_first_sum(f, x, yr, slot):
        total = f[y] + x[y].astype(F32)
        for d in (1, 3, 2):
            net.arrived(yr.at[d - 1], slot + d - 1)
            total = total + yr[d - 1].astype(F32)
        return total

    def y_first_block(out, zz, sums):
        f, p, yr, slot = sums
        hi, yi = zz // NY, lax.rem(zz, NY)
        f[hi, yi] = out

        @pl.when(yi != y)
        def _():
            p[hi, yi] = out.astype(BF16)
            d = lax.rem(yi - y + NY, NY) - 1
            net.aside(p.at[hi, yi], yr.at[d, hi], slot + 2 * d + hi, dev(h, yi, z, k, l))

    def y_first_pass(f, yr, s, x, slot):
        total = f[1 - h, y]
        for d in (1, 3, 2):
            net.arrived(yr.at[d - 1, 1 - h], slot + 2 * (d - 1) + 1 - h)
            total = total + yr[d - 1, 1 - h].astype(F32)
        s[...] = total.astype(BF16)
        first = net.slots()
        net.put(s, x, first, over_x)
        return first

    def y_first_sum(f, yr, x, slot1, slot2):
        total = f[h, y]
        for d in (1, 3, 2):
            net.arrived(yr.at[d - 1, h], slot1 + 2 * (d - 1) + h)
            total = total + yr[d - 1, h].astype(F32)
        net.arrived(x, slot2)
        return total + x[...].astype(F32)

    net.late_first = net.n_recv
    g1, u1, h11, h21 = net.slots(4), net.slots(6), net.slots(4), net.slots(6)
    g2 = net.slots(3)

    def block_gu(zz):
        a = gathered(tok_g, zz)
        y_first_block(dot(a, wu[...]), zz, (u_f, u_p, u_y, u1))
        x_first_block(dot(a, wg[...]), zz, (g_f, g_p, g_x, g1))

    def relay_g(zz):
        x_first_relay(zz, (g_f, g_p, g_x, g1), (g_s, g_y, g2, 36))

    def block_h(zz):
        a = gathered(go_g, zz)
        y_first_block(dot_last(a, wd[CUT:]), zz, (h2_f, h2_p, h2_y, h21))
        x_first_block(dot_last(a, wd[:CUT]), zz, (h1_f, h1_p, h1_x, h11))

    def chips(step):
        return (zs(-side * step), zs(side * step)) if step < 4 else (zs(4),)

    gather_start(tok, tok_g)
    gather_share(tok_g)
    gather_start(go, go_g)
    for c in loads:
        c.wait()
    block_gu(z)
    gather_two(tok_g)
    gather_one(tok_g)
    for zz in chips(1) + chips(2):
        block_gu(zz)
    gather_rest(tok_g)
    gather_share(go_g)
    for zz in chips(3) + chips(4):
        block_gu(zz)
    for zz in (z,) + chips(1):
        relay_g(zz)
    gather_two(go_g)
    for zz in chips(2) + chips(3):
        relay_g(zz)
    gather_one(go_g)
    gather_rest(go_g)

    def h_blocks(lo, hi):
        for zz in ((z,) + chips(1) + chips(2) + chips(3) + chips(4))[lo:hi]:
            block_h(zz)

    h_blocks(0, 3)
    relay_g(zs(4))
    u2 = y_first_pass(u_f, u_y, u_s, u_x, u1)
    h_blocks(3, 8)
    tok_t[...] = flat(tok_a[...]).T
    gate = x_first_sum(g_f, g_x, g_y, g2)
    up = y_first_sum(u_f, u_y, u_x, u1, u2)
    sig = jax.nn.sigmoid(gate)
    gate_v[...] = gate
    up_v[...] = up
    sig_v[...] = sig
    hid_a[0, h, y] = (gate * sig * up).astype(BF16)

    class Spread:
        def __init__(self, buf, lo, hi):
            self.buf, self.cols = buf, pl.ds(lo, hi - lo)
            self.base = net.slots(10)
            self.put(h, y, over_x)
            self.put(h, y, over_y[1])
            self.put(h, y, over_y[3])

        def at(self, hh, yy, half=None):
            rows = pl.ds(0, 96) if half is None else pl.ds(48 * half, 48)
            return self.buf.at[:, hh, yy, rows, self.cols]

        def slot(self, hh, yy, half=None):
            return self.base + (8 + hh if half == 1 else hh * NY + yy)

        def put(self, hh, yy, to, half=None):
            ref = self.at(hh, yy, half)
            net.put(ref, ref, self.slot(hh, yy, half), to)

        def wait(self, hh, yy, half=None):
            net.arrived(self.at(hh, yy, half), self.slot(hh, yy, half))

        def across(self, hh, also_x=False):
            for d, half in ((3, 0), (1, 1)):
                self.wait(hh, ys(d))
                self.put(hh, ys(d), over_y[4 - d], half)
                if also_x:
                    self.put(hh, ys(d), over_x)

    class XThenY(Spread):
        def relay1(self):
            self.wait(1 - h, y)
            self.put(1 - h, y, over_y[1])
            self.put(1 - h, y, over_y[3])

        def relay2(self):
            self.across(h)

        def relay3(self):
            self.across(1 - h)

        def rest(self):
            for hh in (h, 1 - h):
                for half in (0, 1):
                    self.wait(hh, ys(2), half)

    class YThenX(Spread):
        def relay1(self):
            self.across(h, True)

        def relay2(self):
            for half in (0, 1):
                self.wait(h, ys(2), half)
                self.put(h, ys(2), over_x, half)

        def rest(self):
            for d in (0, 1, 3):
                self.wait(1 - h, ys(d))
            for half in (0, 1):
                self.wait(1 - h, ys(2), half)

    width = hid_a.shape[-1]
    hid, gg, gu = hid_a.at[0], gr_a.at[0], gr_a.at[1]

    def grads(at, total):
        gate, up, sig = gate_v[:, at], up_v[:, at], sig_v[:, at]
        gr_a[1, h, y, :, at] = (total * gate * sig).astype(BF16)
        gr_a[0, h, y, :, at] = (total * up * sig * (1.0 + gate * (1.0 - sig))).astype(BF16)

    def weight_grad(left, buf, first, lo, hi, mine):
        at, to = pl.ds(lo, hi - lo), pl.ds(first + lo, hi - lo)
        base = (l if mine else 1 - l) * 320
        right = buf[:, :, :, at].reshape((8 * 96, hi - lo))
        for q in range(2):
            out = dot(left[pl.ds(pl.multiple_of(base + q * 160, 32), 160)], right)
            if mine:
                gw_f[pl.ds(q * 160, 160), to] = out
            else:
                gw_s[pl.ds(q * 160, 160), to] = out.astype(BF16)
        if not mine:
            slot = net.slots()
            net.put(gw_s.at[:, to], gw_r.at[:, to], slot, twin)
            return slot, to

    def weight_out(out, lo, hi, sent):
        slot, at = sent
        net.arrived(gw_r.at[:, at], slot)
        out[:, pl.ds(lo, hi - lo)] = (gw_f[:, at] + gw_r[:, at].astype(F32)).astype(BF16)

    def pair_send(part, pair, lo, hi):
        slot, at = net.slots(), pl.ds(lo, hi - lo)
        net.put(part.at[at, 1 - k], pair.at[at], slot, core)
        return slot, at

    def pair_pass(sums, sent, i, first_sem):
        part, pair, zsend, zrecv, base = sums
        slot, at = sent
        net.arrived(pair.at[at], slot)
        for zz in (2 * i, 2 * i + 1):
            zsend[zz] = (part[zz, k] + pair[zz]).astype(BF16)
            d = lax.rem(zz - z + NZ, NZ)

            @pl.when(d != 0)
            def _():
                net.aside(zsend.at[zz], zrecv.at[d], base + d, dev(h, y, zz, k, l), first_sem + zz)

    def pair_sent(sums, first_sem):
        part, pair, zsend, zrecv, base = sums
        for zz in range(NZ):

            @pl.when(zz != z)
            def _():
                net.aside_sent(zsend.at[zz], zrecv.at[0], base, twin, first_sem + zz)

    def z_sum(sums, out):
        part, pair, zsend, zrecv, slot = sums
        total = part[z, k] + pair[z]
        for d in (1, 7, 2, 6, 3, 5, 4):
            net.arrived(zrecv.at[d], slot + d)
            total = total + zrecv[d].astype(F32)
        zrecv[0] = total.astype(BF16)
        net.put_or_keep(zrecv.at[0], out, slot, twin, h)
        return out, slot

    def rows4(buf, i, at):
        return buf[i // 2, pl.ds(2 * (i % 2), 2), :, at].reshape((192, -1))

    def token_grad(i, lo, hi):
        at = pl.ds(lo, hi - lo)
        out = dot_last(rows4(gg, i, at), wg[:, at]) + dot_last(rows4(gu, i, at), wu[:, at])
        return out.reshape((2, 2, 48, -1))

    sums1 = part1, pair1, zs1, zr1, net.slots(NZ)
    sums2 = part2, pair2, zs2, zr2, net.slots(NZ)

    def mixed_parts():
        sent = []
        for i in range(4):
            out = dot(rows4(hid, i, pl.ds(0, width)), wd[...])
            part1[pl.ds(2 * i, 2)] = out.reshape((2, 2, 48, -1))
            sent.append(pair_send(part1, pair1, 2 * i, 2 * i + 2))
        return sent

    def mixed_pass():
        for i in range(4):
            pair_pass(sums1, sent1[i], i, 20)

    def token_parts():
        sent = []
        for i in range(4):
            part2[pl.ds(2 * i, 2)] += token_grad(i, CUT, width)
            sent.append(pair_send(part2, pair2, 2 * i, 2 * i + 2))
            if i > 1:
                pair_pass(sums2, sent[i - 2], i - 2, 28)
        pair_pass(sums2, sent[2], 2, 28)
        pair_pass(sums2, sent[3], 3, 28)

    hid0 = XThenY(hid_a, 0, CUT)
    hid1 = YThenX(hid_a, CUT, width)
    h12 = x_first_pass(h1_f, h1_x, h1_s, h1_y, h11)
    h22 = y_first_pass(h2_f, h2_y, h2_s, h2_x, h21)
    go_t[...] = flat(go_a[...]).T
    hid0.relay1()
    hid1.relay1()
    hid0.relay2()
    grads(pl.ds(0, CUT), x_first_sum(h1_f, h1_x, h1_y, h12))
    gr0 = XThenY(gr_a, 0, 256)
    gr1 = YThenX(gr_a, 256, CUT)
    grads(pl.ds(CUT, width - CUT), y_first_sum(h2_f, h2_y, h2_x, h21, h22))
    hid1.relay2()
    hid0.relay3()
    gr0.relay1()
    hid0.rest()
    dw0 = weight_grad(go_t, hid, 2 * width, 0, CUT, False)
    hid1.rest()
    dw1 = weight_grad(go_t, hid, 2 * width, CUT, width, False)
    gr1.relay1()
    gr0.relay2()
    gr2 = XThenY(gr_a, CUT, 768)
    gr3 = YThenX(gr_a, 768, width)
    gr1.relay2()
    gr0.relay3()
    sent1 = mixed_parts()
    gr2.relay1()
    gr3.relay1()
    gr2.relay2()
    mixed_pass()
    gr0.rest()
    gr1.rest()
    wg0 = weight_grad(tok_t, gg, 0, 0, CUT, False)
    wu0 = weight_grad(tok_t, gu, width, 0, CUT, False)
    gr3.relay2()
    gr2.relay3()
    for i in range(4):
        part2[pl.ds(2 * i, 2)] = token_grad(i, 0, CUT)
    gr2.rest()
    gr3.rest()
    token_parts()
    wg1 = weight_grad(tok_t, gg, 0, CUT, width, False)
    wu1 = weight_grad(tok_t, gu, width, CUT, width, False)
    for first, n, p, x in (
        (g1, 4, g_p.at[0], g_x.at[0]),
        (u1, 6, u_p.at[0, 0], u_y.at[0, 0]),
        (h11, 4, h1_p.at[0], h1_x.at[0]),
        (h21, 6, h2_p.at[0, 0], h2_y.at[0, 0]),
    ):
        for i in range(n):
            net.aside_sent(p, x, first + i, over_x)
    for d in range(3):
        net.aside_sent(g_s.at[0], g_y.at[0], g2, over_x, 36 + d)
    pair_sent(sums1, 20)
    net.finish(20)
    weight_grad(go_t, hid, 2 * width, 0, width, True)
    weight_out(gwd_o, 0, CUT, dw0)
    weight_out(gwd_o, CUT, width, dw1)
    mixed = z_sum(sums1, mixed_v)
    weight_grad(tok_t, gg, 0, 0, width, True)
    weight_grad(tok_t, gu, width, 0, width, True)
    weight_out(gwg_o, 0, CUT, wg0)
    weight_out(gwu_o, 0, CUT, wu0)
    grad = z_sum(sums2, gt_v)
    weight_out(gwg_o, CUT, width, wg1)
    weight_out(gwu_o, CUT, width, wu1)
    for o, (v, slot) in ((mixed_o, mixed), (gt_o, grad)):
        net.arrived(v, slot)
        o[...] = v[...]
    pair_sent(sums2, 28)
    net.finish()


def copy_out(*refs):
    for i in range(5):
        refs[5 + i][...] = refs[i][...]


def per_device(tokens, w_gate, w_up, w_down, grad_out):
    n_tok, d = tokens.shape
    f = w_gate.shape[1]
    rest = f - CUT

    def x_first(w):
        return [
            pltpu.VMEM((4, 96, w), BF16),
            pltpu.VMEM((4, 96, w), F32),
            pltpu.VMEM((4, 96, w), BF16),
            pltpu.VMEM((4, 96, w), BF16),
            pltpu.VMEM((3, 96, w), BF16),
        ]

    def y_first(w):
        return [
            pltpu.VMEM((2, 4, 96, w), BF16),
            pltpu.VMEM((2, 4, 96, w), F32),
            pltpu.VMEM((3, 2, 96, w), BF16),
            pltpu.VMEM((96, w), BF16),
            pltpu.VMEM((96, w), BF16),
        ]

    scratch = [
        pltpu.VMEM((16, n_tok, d), BF16),
        pltpu.VMEM((16, n_tok, d), BF16),
        pltpu.VMEM(w_gate.shape, BF16),
        pltpu.VMEM(w_up.shape, BF16),
        pltpu.VMEM(w_down.shape, BF16),
        *[pltpu.VMEM((d, 16 * n_tok), BF16)] * 2,
        *x_first(f),
        *y_first(f),
        *x_first(CUT),
        *y_first(rest),
        *[pltpu.VMEM((96, f), F32)] * 3,
        pltpu.VMEM((1, 2, 4, 96, f), BF16),
        pltpu.VMEM((2, 2, 4, 96, f), BF16),
        *[pltpu.VMEM((8, 2, n_tok, d), F32)] * 2,
        *[pltpu.VMEM((8, n_tok, d), F32)] * 2,
        *[pltpu.VMEM((8, n_tok, d), BF16)] * 4,
        *[pltpu.VMEM((n_tok, d), BF16)] * 2,
        pltpu.VMEM((d // 2, 3 * f), F32),
        pltpu.VMEM((d // 2, 3 * f), BF16),
        pltpu.VMEM((d // 2, 3 * f), BF16),
        pltpu.SemaphoreType.DMA((200,)),
        pltpu.SemaphoreType.DMA((40,)),
        pltpu.SemaphoreType.DMA((200,)),
        pltpu.SemaphoreType.DMA((3,)),
    ]
    vmem, hbm = pl.BlockSpec(memory_space=pltpu.VMEM), pl.BlockSpec(memory_space=pl.ANY)
    results = pl.pallas_call(
        kernel,
        out_shape=(
            jax.ShapeDtypeStruct((n_tok, d), BF16),
            jax.ShapeDtypeStruct((n_tok, d), BF16),
            jax.ShapeDtypeStruct((d // 2, f), BF16),
            jax.ShapeDtypeStruct((d // 2, f), BF16),
            jax.ShapeDtypeStruct((d // 2, f), BF16),
        ),
        in_specs=[vmem, hbm, hbm, hbm, vmem],
        out_specs=(vmem,) * 5,
        scratch_shapes=scratch,
        compiler_params=pltpu.CompilerParams(
            collective_id=0, has_side_effects=True, vmem_limit_bytes=62 * 2**20
        ),
        name="swiglu",
    )(tokens, w_gate, w_up, w_down, grad_out)
    mixed, grad_tokens, grad_gate, grad_up, grad_down = pl.pallas_call(
        copy_out,
        out_shape=tuple(jax.ShapeDtypeStruct(r.shape, r.dtype) for r in results),
        in_specs=[vmem] * 5,
        out_specs=(vmem,) * 5,
        name="copy_out",
    )(*results)
    return mixed, grad_tokens, grad_gate, grad_up, grad_down.T


def solution(mesh):
    placed = (
        P(("col", "dp"), "row"),
        P("row", "col"),
        P("row", "col"),
        P("col", "row"),
        P(("col", "dp"), "row"),
    )
    return jax.shard_map(
        per_device,
        mesh=mesh,
        in_specs=placed,
        out_specs=(
            P(("col", "dp"), "row"),
            P(("col", "dp"), "row"),
            P(("row", "dp"), "col"),
            P(("row", "dp"), "col"),
            P("col", ("row", "dp")),
        ),
        check_vma=False,
    )
```

```python
import functools

import jax
import jax.numpy as jnp
from jax import lax
from jax.experimental import pallas as pl
from jax.experimental.pallas import tpu as pltpu
from jax.sharding import PartitionSpec as P

MESH = pl.DeviceIdType.MESH
BF16, F32 = jnp.bfloat16, jnp.float32
NY, NZ = 4, 8
CUT = 512


def dot(a, b):
    return jnp.dot(a, b, preferred_element_type=F32)


def dot_last(a, b):
    return lax.dot_general(a, b, (((1,), (1,)), ((), ())), preferred_element_type=F32)


def dot_first(a, b):
    return lax.dot_general(a, b, (((0,), (0,)), ((), ())), preferred_element_type=F32)


def flat(x):
    return x.reshape((-1, x.shape[-1]))


class Links:
    def __init__(self, send, late, recv):
        self.send, self.late, self.recv = send, late, recv
        self.n_send = self.n_recv = 0
        self.started = []

    def slots(self, n=1):
        first = self.n_recv
        self.n_recv += n
        return first

    def copy(self, src, dst, slot, to):
        c = pltpu.make_async_remote_copy(
            src_ref=src,
            dst_ref=dst,
            send_sem=self.send.at[self.n_send],
            recv_sem=self.recv.at[slot],
            device_id=to,
            device_id_type=MESH,
        )
        self.n_send += 1
        return c

    def put(self, src, dst, slot, to):
        c = self.copy(src, dst, slot, to)
        c.start()
        self.started.append((c, None))

    def put_or_keep(self, src, dst, slot, to, away):
        c = self.copy(src, dst, slot, to)

        @pl.when(away == 1)
        def _():
            c.start()

        @pl.when(away == 0)
        def _():
            pltpu.make_async_copy(src, dst, self.recv.at[slot]).start()

        self.started.append((c, away))

    def aside(self, src, dst, slot, to, sem=None):
        pltpu.make_async_remote_copy(
            src_ref=src,
            dst_ref=dst,
            send_sem=self.late.at[slot - self.late_first if sem is None else sem],
            recv_sem=self.recv.at[slot],
            device_id=to,
            device_id_type=MESH,
        ).start()

    def aside_sent(self, src, dst, slot, to, sem=None):
        pltpu.make_async_remote_copy(
            src_ref=src,
            dst_ref=dst,
            send_sem=self.late.at[slot - self.late_first if sem is None else sem],
            recv_sem=self.recv.at[slot],
            device_id=to,
            device_id_type=MESH,
        ).wait_send()

    def arrived(self, dst, slot):
        pltpu.make_async_copy(dst, dst, self.recv.at[slot]).wait()

    def finish(self, last=0):
        done, self.started = self.started[: len(self.started) - last], self.started[len(self.started) - last :]
        for c, away in done:
            if away is None:
                c.wait_send()
            else:
                pl.when(away == 1)(c.wait_send)


def kernel(
    tok, wg_h, wu_h, wd_h, go, mixed_o, gt_o, gwg_o, gwu_o, gwd_o,
    tok_a, go_a, wg, wu, wd, tok_t, go_t,
    g_p, g_f, g_x, g_s, g_y, u_p, u_f, u_y, u_s, u_x,
    h1_p, h1_f, h1_x, h1_s, h1_y, h2_p, h2_f, h2_y, h2_s, h2_x,
    gate_v, up_v, sig_v, hid_a, gr_a,
    part1, part2, pair1, pair2, zs1, zs2, zr1, zr2, mixed_v, gt_v,
    gw_f, gw_s, gw_r,
    send, late, recv, loc,
):
    row, col, l = lax.axis_index("row"), lax.axis_index("col"), lax.axis_index("dp")
    h, y = row // NY, lax.rem(row, NY)
    z, k = col // 2, lax.rem(col, 2)

    def dev(hh, yy, zz, kk, ll):
        return (hh * NY + yy, zz * 2 + kk, ll)

    def ys(d):
        return lax.rem(y + d, NY)

    def zs(d):
        return lax.rem(z + d + NZ, NZ)

    over_y = [None] + [dev(h, ys(d), z, k, l) for d in (1, 2, 3)]
    over_x = dev(1 - h, y, z, k, 1 - l)
    twin = (row, col, 1 - l)
    core = dev(h, y, z, 1 - k, l)

    loads = []
    for i, (src, dst) in enumerate(((wg_h, wg), (wu_h, wu), (wd_h, wd))):
        c = pltpu.make_async_copy(src, dst, loc.at[i])
        c.start()
        loads.append(c)

    barrier = pltpu.get_barrier_semaphore()
    friends = [over_x, twin, core] + over_y[1:]
    for d in (1, 2, 6, 7):
        friends.append(dev(h, y, zs(d), k, l))
    for to in friends:
        pl.semaphore_signal(barrier, inc=1, device_id=to, device_id_type=MESH)
    pl.semaphore_wait(barrier, len(friends))

    net = Links(send, late, recv)

    side = 1 - 2 * k
    tok_g, go_g = [(dst, net.slots(16)) for dst in (tok_a, go_a)]

    def gather_put(gather, origin, to):
        dst, base = gather
        net.put(dst.at[origin], dst.at[origin], base + origin, to)

    def gather_start(src, gather):
        dst, base = gather
        net.put_or_keep(src, dst.at[col], base + col, twin, h)

    def gather_share(gather):
        dst, base = gather
        net.arrived(dst.at[col], base + col)
        gather_put(gather, col, core)
        for d in (2 * side, -2 * side, side, -side):
            gather_put(gather, col, dev(h, y, zs(d), k, l))

    def gather_pass(gather, steps, targets):
        origin = zs(steps) * 2 + k
        dst, base = gather
        net.arrived(dst.at[origin], base + origin)
        for d in targets:
            gather_put(gather, origin, dev(h, y, zs(d), k, l))
        gather_put(gather, origin, core)

    def gather_two(gather):
        gather_pass(gather, -2 * side, (2 * side, side))
        gather_pass(gather, 2 * side, (-side,))

    def gather_one(gather):
        gather_pass(gather, -side, ())
        gather_pass(gather, side, ())

    def gather_rest(gather):
        for d in (-3 * side, 3 * side, 4):
            gather_pass(gather, d, ())

    def gathered(gather, zz):
        dst, base = gather
        other = zz * 2 + 1 - k
        net.arrived(dst.at[other], base + other)
        return flat(dst[pl.ds(zz * 2, 2)])

    def x_first_block(out, zz, sums):
        f, p, x, slot = sums
        hi, yi = zz // NY, lax.rem(zz, NY)

        @pl.when(hi == h)
        def _():
            f[yi] = out

        @pl.when(hi != h)
        def _():
            p[yi] = out.astype(BF16)
            net.aside(p.at[yi], x.at[yi], slot + yi, over_x)

    def x_first_pass(f, x, s, yr, slot):
        first = net.slots(3)
        for d in (2, 1, 3):
            i = ys(d)
            net.arrived(x.at[i], slot + i)
            s[i] = (f[i] + x[i].astype(F32)).astype(BF16)
            net.put(s.at[i], yr.at[d - 1], first + d - 1, over_y[d])
        net.arrived(x.at[y], slot + y)
        return first

    def x_first_relay(zz, sums, to):
        f, p, x, slot = sums
        s, yr, first, sem = to
        hi, yi = zz // NY, lax.rem(zz, NY)

        @pl.when(hi == h)
        def _():
            net.arrived(x.at[yi], slot + yi)

            @pl.when(yi != y)
            def _():
                d = lax.rem(yi - y + NY, NY) - 1
                s[yi] = (f[yi] + x[yi].astype(F32)).astype(BF16)
                net.aside(s.at[yi], yr.at[d], first + d, dev(h, yi, z, k, l), sem + d)

    def x_first_sum(f, x, yr, slot):
        total = f[y] + x[y].astype(F32)
        for d in (1, 3, 2):
            net.arrived(yr.at[d - 1], slot + d - 1)
            total = total + yr[d - 1].astype(F32)
        return total

    def y_first_block(out, zz, sums):
        f, p, yr, slot = sums
        hi, yi = zz // NY, lax.rem(zz, NY)
        f[hi, yi] = out

        @pl.when(yi != y)
        def _():
            p[hi, yi] = out.astype(BF16)
            d = lax.rem(yi - y + NY, NY) - 1
            net.aside(p.at[hi, yi], yr.at[d, hi], slot + 2 * d + hi, dev(h, yi, z, k, l))

    def y_first_pass(f, yr, s, x, slot):
        total = f[1 - h, y]
        for d in (1, 3, 2):
            net.arrived(yr.at[d - 1, 1 - h], slot + 2 * (d - 1) + 1 - h)
            total = total + yr[d - 1, 1 - h].astype(F32)
        s[...] = total.astype(BF16)
        first = net.slots()
        net.put(s, x, first, over_x)
        return first

    def y_first_sum(f, yr, x, slot1, slot2):
        total = f[h, y]
        for d in (1, 3, 2):
            net.arrived(yr.at[d - 1, h], slot1 + 2 * (d - 1) + h)
            total = total + yr[d - 1, h].astype(F32)
        net.arrived(x, slot2)
        return total + x[...].astype(F32)

    net.late_first = net.n_recv
    g1, u1, h11, h21 = net.slots(4), net.slots(6), net.slots(4), net.slots(6)
    g2 = net.slots(3)

    def block_gu(zz):
        a = gathered(tok_g, zz)
        y_first_block(dot(a, wu[...]), zz, (u_f, u_p, u_y, u1))
        x_first_block(dot(a, wg[...]), zz, (g_f, g_p, g_x, g1))

    def relay_g(zz):
        x_first_relay(zz, (g_f, g_p, g_x, g1), (g_s, g_y, g2, 36))

    def block_h(zz):
        a = gathered(go_g, zz)
        y_first_block(dot_last(a, wd[CUT:]), zz, (h2_f, h2_p, h2_y, h21))
        x_first_block(dot_last(a, wd[:CUT]), zz, (h1_f, h1_p, h1_x, h11))

    def chips(step):
        return (zs(-side * step), zs(side * step)) if step < 4 else (zs(4),)

    gather_start(tok, tok_g)
    gather_share(tok_g)
    gather_start(go, go_g)
    for c in loads:
        c.wait()
    block_gu(z)
    gather_two(tok_g)
    gather_one(tok_g)
    for zz in chips(1) + chips(2):
        block_gu(zz)
    gather_rest(tok_g)
    gather_share(go_g)
    for zz in chips(3) + chips(4):
        block_gu(zz)
    for zz in (z,) + chips(1):
        relay_g(zz)
    gather_two(go_g)
    for zz in chips(2) + chips(3):
        relay_g(zz)
    gather_one(go_g)
    gather_rest(go_g)

    def h_blocks(lo, hi):
        for zz in ((z,) + chips(1) + chips(2) + chips(3) + chips(4))[lo:hi]:
            block_h(zz)

    h_blocks(0, 3)
    relay_g(zs(4))
    u2 = y_first_pass(u_f, u_y, u_s, u_x, u1)
    h_blocks(3, 8)
    tok_t[...] = flat(tok_a[...]).T
    gate = x_first_sum(g_f, g_x, g_y, g2)
    up = y_first_sum(u_f, u_y, u_x, u1, u2)
    sig = jax.nn.sigmoid(gate)
    gate_v[...] = gate
    up_v[...] = up
    sig_v[...] = sig
    hid_a[0, h, y] = (gate * sig * up).astype(BF16)

    class Spread:
        def __init__(self, buf, lo, hi):
            self.buf, self.cols = buf, pl.ds(lo, hi - lo)
            self.base = net.slots(10)
            self.put(h, y, over_x)
            self.put(h, y, over_y[1])
            self.put(h, y, over_y[3])

        def at(self, hh, yy, half=None):
            rows = pl.ds(0, 96) if half is None else pl.ds(48 * half, 48)
            return self.buf.at[:, hh, yy, rows, self.cols]

        def slot(self, hh, yy, half=None):
            return self.base + (8 + hh if half == 1 else hh * NY + yy)

        def put(self, hh, yy, to, half=None):
            ref = self.at(hh, yy, half)
            net.put(ref, ref, self.slot(hh, yy, half), to)

        def wait(self, hh, yy, half=None):
            net.arrived(self.at(hh, yy, half), self.slot(hh, yy, half))

        def across(self, hh, also_x=False):
            for d, half in ((3, 0), (1, 1)):
                self.wait(hh, ys(d))
                self.put(hh, ys(d), over_y[4 - d], half)
                if also_x:
                    self.put(hh, ys(d), over_x)

    class XThenY(Spread):
        def relay1(self):
            self.wait(1 - h, y)
            self.put(1 - h, y, over_y[1])
            self.put(1 - h, y, over_y[3])

        def relay2(self):
            self.across(h)

        def relay3(self):
            self.across(1 - h)

        def rest(self):
            for hh in (h, 1 - h):
                for half in (0, 1):
                    self.wait(hh, ys(2), half)

    class YThenX(Spread):
        def relay1(self):
            self.across(h, True)

        def relay2(self):
            for half in (0, 1):
                self.wait(h, ys(2), half)
                self.put(h, ys(2), over_x, half)

        def rest(self):
            for d in (0, 1, 3):
                self.wait(1 - h, ys(d))
            for half in (0, 1):
                self.wait(1 - h, ys(2), half)

    width = hid_a.shape[-1]
    hid, gg, gu = hid_a.at[0], gr_a.at[0], gr_a.at[1]

    def grads(at, total):
        gate, up, sig = gate_v[:, at], up_v[:, at], sig_v[:, at]
        gr_a[1, h, y, :, at] = (total * gate * sig).astype(BF16)
        gr_a[0, h, y, :, at] = (total * up * sig * (1.0 + gate * (1.0 - sig))).astype(BF16)

    def weight_grad(left, buf, first, lo, hi, mine):
        at, to = pl.ds(lo, hi - lo), pl.ds(first + lo, hi - lo)
        base = (l if mine else 1 - l) * 320
        right = buf[:, :, :, at].reshape((8 * 96, hi - lo))
        for q in range(2):
            out = dot(left[pl.ds(pl.multiple_of(base + q * 160, 32), 160)], right)
            if mine:
                gw_f[pl.ds(q * 160, 160), to] = out
            else:
                gw_s[pl.ds(q * 160, 160), to] = out.astype(BF16)
        if not mine:
            slot = net.slots()
            net.put(gw_s.at[:, to], gw_r.at[:, to], slot, twin)
            return slot, to

    def weight_out(out, lo, hi, sent):
        slot, at = sent
        net.arrived(gw_r.at[:, at], slot)
        out[:, pl.ds(lo, hi - lo)] = (gw_f[:, at] + gw_r[:, at].astype(F32)).astype(BF16)

    def pair_send(part, pair, lo, hi):
        slot, at = net.slots(), pl.ds(lo, hi - lo)
        net.put(part.at[at, 1 - k], pair.at[at], slot, core)
        return slot, at

    def pair_pass(sums, sent, i, first_sem):
        part, pair, zsend, zrecv, base = sums
        slot, at = sent
        net.arrived(pair.at[at], slot)
        for zz in (2 * i, 2 * i + 1):
            zsend[zz] = (part[zz, k] + pair[zz]).astype(BF16)
            d = lax.rem(zz - z + NZ, NZ)

            @pl.when(d != 0)
            def _():
                net.aside(zsend.at[zz], zrecv.at[d], base + d, dev(h, y, zz, k, l), first_sem + zz)

    def pair_sent(sums, first_sem):
        part, pair, zsend, zrecv, base = sums
        for zz in range(NZ):

            @pl.when(zz != z)
            def _():
                net.aside_sent(zsend.at[zz], zrecv.at[0], base, twin, first_sem + zz)

    def z_sum(sums, out):
        part, pair, zsend, zrecv, slot = sums
        total = part[z, k] + pair[z]
        for d in (1, 7, 2, 6, 3, 5, 4):
            net.arrived(zrecv.at[d], slot + d)
            total = total + zrecv[d].astype(F32)
        zrecv[0] = total.astype(BF16)
        net.put_or_keep(zrecv.at[0], out, slot, twin, h)
        return out, slot

    def rows4(buf, i, at):
        return buf[i // 2, pl.ds(2 * (i % 2), 2), :, at].reshape((192, -1))

    def token_grad(i, lo, hi):
        at = pl.ds(lo, hi - lo)
        out = dot_last(rows4(gg, i, at), wg[:, at]) + dot_last(rows4(gu, i, at), wu[:, at])
        return out.reshape((2, 2, 48, -1))

    sums1 = part1, pair1, zs1, zr1, net.slots(NZ)
    sums2 = part2, pair2, zs2, zr2, net.slots(NZ)

    def mixed_parts():
        sent = []
        for i in range(4):
            out = dot(rows4(hid, i, pl.ds(0, width)), wd[...])
            part1[pl.ds(2 * i, 2)] = out.reshape((2, 2, 48, -1))
            sent.append(pair_send(part1, pair1, 2 * i, 2 * i + 2))
        return sent

    def mixed_pass():
        for i in range(4):
            pair_pass(sums1, sent1[i], i, 20)

    def token_parts():
        sent = []
        for i in range(4):
            part2[pl.ds(2 * i, 2)] += token_grad(i, CUT, width)
            sent.append(pair_send(part2, pair2, 2 * i, 2 * i + 2))
            if i > 1:
                pair_pass(sums2, sent[i - 2], i - 2, 28)
        pair_pass(sums2, sent[2], 2, 28)
        pair_pass(sums2, sent[3], 3, 28)

    hid0 = XThenY(hid_a, 0, CUT)
    hid1 = YThenX(hid_a, CUT, width)
    h12 = x_first_pass(h1_f, h1_x, h1_s, h1_y, h11)
    h22 = y_first_pass(h2_f, h2_y, h2_s, h2_x, h21)
    go_t[...] = flat(go_a[...]).T
    hid0.relay1()
    hid1.relay1()
    hid0.relay2()
    grads(pl.ds(0, CUT), x_first_sum(h1_f, h1_x, h1_y, h12))
    gr0 = XThenY(gr_a, 0, 256)
    gr1 = YThenX(gr_a, 256, CUT)
    grads(pl.ds(CUT, width - CUT), y_first_sum(h2_f, h2_y, h2_x, h21, h22))
    hid1.relay2()
    hid0.relay3()
    hid0.rest()
    dw0 = weight_grad(go_t, hid, 2 * width, 0, CUT, False)
    hid1.rest()
    dw1 = weight_grad(go_t, hid, 2 * width, CUT, width, False)
    gr0.relay1()
    gr1.relay1()
    gr0.relay2()
    gr2 = XThenY(gr_a, CUT, 768)
    gr3 = YThenX(gr_a, 768, width)
    gr1.relay2()
    gr0.relay3()
    sent1 = mixed_parts()
    gr2.relay1()
    gr3.relay1()
    gr2.relay2()
    mixed_pass()
    gr0.rest()
    gr1.rest()
    wg0 = weight_grad(tok_t, gg, 0, 0, CUT, False)
    wu0 = weight_grad(tok_t, gu, width, 0, CUT, False)
    gr3.relay2()
    gr2.relay3()
    for i in range(4):
        part2[pl.ds(2 * i, 2)] = token_grad(i, 0, CUT)
    gr2.rest()
    gr3.rest()
    token_parts()
    wg1 = weight_grad(tok_t, gg, 0, CUT, width, False)
    wu1 = weight_grad(tok_t, gu, width, CUT, width, False)
    for first, n, p, x in (
        (g1, 4, g_p.at[0], g_x.at[0]),
        (u1, 6, u_p.at[0, 0], u_y.at[0, 0]),
        (h11, 4, h1_p.at[0], h1_x.at[0]),
        (h21, 6, h2_p.at[0, 0], h2_y.at[0, 0]),
    ):
        for i in range(n):
            net.aside_sent(p, x, first + i, over_x)
    for d in range(3):
        net.aside_sent(g_s.at[0], g_y.at[0], g2, over_x, 36 + d)
    pair_sent(sums1, 20)
    net.finish(20)
    weight_grad(go_t, hid, 2 * width, 0, width, True)
    weight_out(gwd_o, 0, CUT, dw0)
    weight_out(gwd_o, CUT, width, dw1)
    mixed = z_sum(sums1, mixed_v)
    weight_grad(tok_t, gg, 0, 0, width, True)
    weight_grad(tok_t, gu, width, 0, width, True)
    weight_out(gwg_o, 0, CUT, wg0)
    weight_out(gwu_o, 0, CUT, wu0)
    grad = z_sum(sums2, gt_v)
    weight_out(gwg_o, CUT, width, wg1)
    weight_out(gwu_o, CUT, width, wu1)
    for o, (v, slot) in ((mixed_o, mixed), (gt_o, grad)):
        net.arrived(v, slot)
        o[...] = v[...]
    pair_sent(sums2, 28)
    net.finish()


def copy_out(*refs):
    for i in range(5):
        refs[5 + i][...] = refs[i][...]


def per_device(tokens, w_gate, w_up, w_down, grad_out):
    n_tok, d = tokens.shape
    f = w_gate.shape[1]
    rest = f - CUT

    def x_first(w):
        return [
            pltpu.VMEM((4, 96, w), BF16),
            pltpu.VMEM((4, 96, w), F32),
            pltpu.VMEM((4, 96, w), BF16),
            pltpu.VMEM((4, 96, w), BF16),
            pltpu.VMEM((3, 96, w), BF16),
        ]

    def y_first(w):
        return [
            pltpu.VMEM((2, 4, 96, w), BF16),
            pltpu.VMEM((2, 4, 96, w), F32),
            pltpu.VMEM((3, 2, 96, w), BF16),
            pltpu.VMEM((96, w), BF16),
            pltpu.VMEM((96, w), BF16),
        ]

    scratch = [
        pltpu.VMEM((16, n_tok, d), BF16),
        pltpu.VMEM((16, n_tok, d), BF16),
        pltpu.VMEM(w_gate.shape, BF16),
        pltpu.VMEM(w_up.shape, BF16),
        pltpu.VMEM(w_down.shape, BF16),
        *[pltpu.VMEM((d, 16 * n_tok), BF16)] * 2,
        *x_first(f),
        *y_first(f),
        *x_first(CUT),
        *y_first(rest),
        *[pltpu.VMEM((96, f), F32)] * 3,
        pltpu.VMEM((1, 2, 4, 96, f), BF16),
        pltpu.VMEM((2, 2, 4, 96, f), BF16),
        *[pltpu.VMEM((8, 2, n_tok, d), F32)] * 2,
        *[pltpu.VMEM((8, n_tok, d), F32)] * 2,
        *[pltpu.VMEM((8, n_tok, d), BF16)] * 4,
        *[pltpu.VMEM((n_tok, d), BF16)] * 2,
        pltpu.VMEM((d // 2, 3 * f), F32),
        pltpu.VMEM((d // 2, 3 * f), BF16),
        pltpu.VMEM((d // 2, 3 * f), BF16),
        pltpu.SemaphoreType.DMA((200,)),
        pltpu.SemaphoreType.DMA((40,)),
        pltpu.SemaphoreType.DMA((200,)),
        pltpu.SemaphoreType.DMA((3,)),
    ]
    vmem, hbm = pl.BlockSpec(memory_space=pltpu.VMEM), pl.BlockSpec(memory_space=pl.ANY)
    results = pl.pallas_call(
        kernel,
        out_shape=(
            jax.ShapeDtypeStruct((n_tok, d), BF16),
            jax.ShapeDtypeStruct((n_tok, d), BF16),
            jax.ShapeDtypeStruct((d // 2, f), BF16),
            jax.ShapeDtypeStruct((d // 2, f), BF16),
            jax.ShapeDtypeStruct((d // 2, f), BF16),
        ),
        in_specs=[vmem, hbm, hbm, hbm, vmem],
        out_specs=(vmem,) * 5,
        scratch_shapes=scratch,
        compiler_params=pltpu.CompilerParams(
            collective_id=0, has_side_effects=True, vmem_limit_bytes=62 * 2**20
        ),
        name="swiglu",
    )(tokens, w_gate, w_up, w_down, grad_out)
    mixed, grad_tokens, grad_gate, grad_up, grad_down = pl.pallas_call(
        copy_out,
        out_shape=tuple(jax.ShapeDtypeStruct(r.shape, r.dtype) for r in results),
        in_specs=[vmem] * 5,
        out_specs=(vmem,) * 5,
        name="copy_out",
    )(*results)
    return mixed, grad_tokens, grad_gate, grad_up, grad_down.T


def solution(mesh):
    placed = (
        P(("col", "dp"), "row"),
        P("row", "col"),
        P("row", "col"),
        P("col", "row"),
        P(("col", "dp"), "row"),
    )
    return jax.shard_map(
        per_device,
        mesh=mesh,
        in_specs=placed,
        out_specs=(
            P(("col", "dp"), "row"),
            P(("col", "dp"), "row"),
            P(("row", "dp"), "col"),
            P(("row", "dp"), "col"),
            P("col", ("row", "dp")),
        ),
        check_vma=False,
    )
```
